32 devices in a mesh: groups: 2 (over x), surf: 16 (over z, y, core).
Axes of the slice: x: 2, y: 2, z: 4, core: 2. Of those that a mesh axis runs over, the one named last changes fastest.
Arguments:
- sensitivity: bfloat16 [96, 131072], P(None, ('groups', 'surf')), parts along dimension 1, may hold values from -6 to 6
- owner: int32 [131072], P(('groups', 'surf')), parts along dimension 0, may hold values from 0 to 65535, as said below
- patch_count: int32 [32], P(('groups', 'surf')), parts along dimension 0, may hold values from 16 to 32, as said below
- neighbours: int32 [1024, 9], P(('groups', 'surf')), parts along dimension 0, may hold values from 0 to 511, as said below
- coupling: float32 [1024, 9], P(('groups', 'surf')), parts along dimension 0, may hold values from 0.25 to 2
Outputs:
- surface_grad: float32 [96, 131072], P(None, ('groups', 'surf')), parts along dimension 1
- smoothed: float32 [96, 131072], P(None, ('groups', 'surf')), parts along dimension 1
The draws below stay inside these ranges and needn't reach their ends.
There are 2 independent parts, one for each index of `groups`. The reference program is written for one: setup_inputs(seed, part) draws one part's arguments, and reference() takes and returns one part's arrays. A program takes and returns all parts, laid end to end along the dimension named above; each array names one. Nothing has to cross between parts.
Inputs may be any that keep to these rules, and one draw needn't show every extreme that they name: Each face's owner lies in the node range of its own partition or of a partition beside it, 4096 nodes a partition. `patch_count`: the first partition is full. `neighbours`: each neighbour differs from its patch by 1 to 4 in patch order.
All inputs are finite; a program needn't handle non-finite values.
Results may differ from the reference program's by a relative error of at most 0.0003.
Values may be sent and summed in bfloat16 or wider, within the bound.
A program may use at most 64 MiB of HBM per device.

```python
import math
import jax
import jax.numpy as jnp

COLS = 96
NODES = 128
NBR = 9
REACH = 4
SWEEPS = 4
PATCH_DEV = 32
FACE_DEV = 4096
PARTITIONS = 16
NPATCH = 512
FACES = 65536


def draw_owner(key, part):
    partitions = FACES // FACE_DEV
    faces_ids = jnp.arange(FACES, dtype=jnp.int32)
    home = faces_ids // FACE_DEV
    first_key, second_key = jax.random.split(key)
    delta = jax.random.randint(first_key, (FACES,), -1, 2, dtype=jnp.int32)
    target = home + delta
    target = jnp.where((target < 0) | (target >= partitions), home, target)
    span = PATCH_DEV * NODES
    return target * span + jax.random.randint(second_key, (FACES,), 0, span, dtype=jnp.int32)


def draw_patch_count(key, part):
    counts = jax.random.randint(key, (PARTITIONS,), (PATCH_DEV + 1) // 2, PATCH_DEV + 1, dtype=jnp.int32)
    return counts.at[0].set(PATCH_DEV)


def draw_neighbours(key, part):
    first_key, second_key = jax.random.split(jax.random.fold_in(key, 7))
    patch_ids = jnp.arange(NPATCH, dtype=jnp.int32)[:, None]
    offsets = jax.random.randint(first_key, (NPATCH, NBR), 1, REACH + 1, dtype=jnp.int32)
    offsets = offsets.at[:, 0].set(REACH)
    signs = 2 * jax.random.randint(second_key, (NPATCH, NBR), 0, 2, dtype=jnp.int32) - 1
    chosen = patch_ids + signs * offsets
    flipped = patch_ids - signs * offsets
    return jnp.where((chosen < 0) | (chosen >= NPATCH), flipped, chosen)


def block_levels(rng, dims, cuts, low, high):
    level = 1.0
    for axis_at, parts in cuts:
        draws = jax.random.uniform(jax.random.fold_in(jax.random.fold_in(rng, 6), axis_at), (parts,), jnp.float32, low / len(cuts), high / len(cuts))
        level = level * jnp.repeat(jnp.exp(draws), dims[axis_at] // parts).reshape((-1,) + (1,) * (len(dims) - 1 - axis_at))
    return level


def bell_draw(own_key, shape, spread, reach, cuts=(), kind=jnp.bfloat16):
    result = jax.random.normal(own_key, shape, jnp.float32) * spread
    if len(cuts) > 0:
        result = block_levels(own_key, shape, cuts, -0.22, 0.18) * result
    return jnp.clip(result, min=-reach, max=reach).astype(kind)


def setup_inputs(seed: int = 0, part: int = 0) -> dict:
    streams_of = jax.random.split(jax.random.key(seed), 6)
    part_splits = jax.random.split(jax.random.fold_in(streams_of[5], part), 6)
    sensitivity = bell_draw(part_splits[0], (COLS, FACES), 1.0, 6.0, ((1, 16),))
    owner = draw_owner(jax.random.fold_in(jax.random.fold_in(streams_of[5], part), 71), part)
    patch_count = draw_patch_count(jax.random.fold_in(jax.random.fold_in(streams_of[5], part), 71), part)
    neighbours = draw_neighbours(jax.random.fold_in(jax.random.fold_in(streams_of[5], part), 71), part)
    coupling = jnp.clip(jnp.exp(math.log(2.0) - 2.0794415 * jax.random.uniform(part_splits[4], (NPATCH, NBR), jnp.float32) ** block_levels(part_splits[4], (NPATCH, NBR), ((0, 16),), -0.2, 0.2)), 0.25, 2.0)
    return dict(sensitivity=sensitivity, owner=owner, patch_count=patch_count, neighbours=neighbours, coupling=coupling)


smoothing = 1.5


def reference(sensitivity, owner, patch_count, neighbours, coupling):
    total_nodes = NPATCH * NODES
    summed = jnp.zeros((COLS, total_nodes), jnp.float32).at[:, owner].add(sensitivity.astype(jnp.float32))
    patch_ids = jnp.arange(NPATCH, dtype=jnp.int32)
    alive = (patch_ids % PATCH_DEV < patch_count[patch_ids // PATCH_DEV]).astype(jnp.float32)
    surface = summed.reshape(COLS, NPATCH, NODES) * alive[None, :, None]
    diagonal = 1.0 + smoothing * (2.0 + jnp.sum(coupling, axis=1))
    field = surface
    for sweep in range(SWEEPS):
        links = jnp.roll(field, 1, axis=2) + jnp.roll(field, -1, axis=2)
        for entry in range(NBR):
            links = links + coupling[:, entry][None, :, None] * jnp.take(field, neighbours[:, entry], axis=1)
        field = alive[None, :, None] * (surface + smoothing * links) / diagonal[None, :, None]
    return surface.reshape(COLS, total_nodes), field.reshape(COLS, total_nodes)
```

```python
import functools

import jax
import jax.numpy as jnp
from jax import lax
from jax.experimental import pallas as pl
from jax.experimental.pallas import tpu as pltpu
from jax.sharding import PartitionSpec as P

NODES = 128
REACH = 4
SWEEPS = 4
LOW = 256
LANES = 128
smoothing = 1.5
OFFSETS = [d for d in range(-REACH, REACH + 1) if d != 0]
NOFF = len(OFFSETS)
MESH = pl.DeviceIdType.MESH


def kernel(
    chunk,
    sens,
    owner,
    count,
    neighbours,
    coupling,
    surface_out,
    smooth_out,
    values,
    owners,
    masked,
    low_hot,
    acc,
    fields,
    weights,
    surface_stage,
    smooth_stage,
    load_sem,
    oload_sem,
    send_sem,
    recv_sem,
    osend_sem,
    orecv_sem,
    hsend_sem,
    hrecv_sem,
    out_sem,
):
    columns, faces = sens.shape
    patches = neighbours.shape[0]
    span = patches * NODES
    highs = span // LOW
    chunks = faces // chunk
    pieces = chunk // LANES
    orow = faces // LANES
    position = lax.axis_index("surf")
    peers = lax.axis_size("surf")
    has_below = position > 0
    has_above = position < peers - 1

    def local_load(k):
        return pltpu.make_async_copy(sens.at[:, pl.ds(k * chunk, chunk)], values.at[0, k], load_sem.at[k])

    def face_copy(side, k):
        target = position + 1 if side == 0 else position - 1
        return pltpu.make_async_remote_copy(
            src_ref=sens.at[:, pl.ds(k * chunk, chunk)],
            dst_ref=values.at[1 + side, k],
            send_sem=send_sem.at[side, k],
            recv_sem=recv_sem.at[side, k],
            device_id={"surf": target},
            device_id_type=MESH,
        )

    def owner_copy(side):
        target = position + 1 if side == 0 else position - 1
        return pltpu.make_async_remote_copy(
            src_ref=owner,
            dst_ref=owners.at[1 + side],
            send_sem=osend_sem.at[side],
            recv_sem=orecv_sem.at[side],
            device_id={"surf": target},
            device_id_type=MESH,
        )

    def halo_copy(side, sweep):
        target = position + 1 if side == 0 else position - 1
        source = patches if side == 0 else REACH
        landing = 0 if side == 0 else patches + REACH
        return pltpu.make_async_remote_copy(
            src_ref=fields.at[sweep, pl.ds(source, REACH)],
            dst_ref=fields.at[sweep, pl.ds(landing, REACH)],
            send_sem=hsend_sem.at[side, sweep],
            recv_sem=hrecv_sem.at[side, sweep],
            device_id={"surf": target},
            device_id_type=MESH,
        )

    own_owner = pltpu.make_async_copy(owner, owners.at[0], oload_sem)
    own_owner.start()
    for k in range(chunks):
        local_load(k).start()

    barrier = pltpu.get_barrier_semaphore()

    @pl.when(has_below)
    def _():
        pl.semaphore_signal(barrier, inc=1, device_id={"surf": position - 1}, device_id_type=MESH)

    @pl.when(has_above)
    def _():
        pl.semaphore_signal(barrier, inc=1, device_id={"surf": position + 1}, device_id_type=MESH)

    both = jnp.logical_and(has_below, has_above)

    @pl.when(both)
    def _():
        pl.semaphore_wait(barrier, 2)

    @pl.when(jnp.logical_not(both))
    def _():
        pl.semaphore_wait(barrier, 1)

    @pl.when(has_above)
    def _():
        owner_copy(0).start()

    @pl.when(has_below)
    def _():
        owner_copy(1).start()

    for k in range(chunks):

        @pl.when(has_above)
        def _(k=k):
            face_copy(0, k).start()

        @pl.when(has_below)
        def _(k=k):
            face_copy(1, k).start()

    slots = lax.broadcasted_iota(jnp.int32, neighbours.shape, 0)
    distance = neighbours[...] - (position * patches + slots)
    links = coupling[...]
    rows = lax.broadcasted_iota(jnp.int32, (patches, LANES), 0)
    alive = jnp.where(rows < count[0], 1.0, 0.0).astype(jnp.float32)
    diagonal = 1.0 + smoothing * (2.0 + jnp.sum(links, axis=1, keepdims=True))
    share = alive / jnp.broadcast_to(diagonal, alive.shape)
    weights[NOFF] = share
    weights[NOFF + 1] = smoothing * share
    weights[NOFF + 2] = alive
    for at, offset in enumerate(OFFSETS):
        total = jnp.sum(jnp.where(distance == offset, links, 0.0), axis=1, keepdims=True)
        weights[at] = smoothing * share * jnp.broadcast_to(total, alive.shape)

    zero_halo = jnp.zeros((REACH, columns, NODES), jnp.float32)

    @pl.when(jnp.logical_not(has_below))
    def _():
        for sweep in range(SWEEPS):
            fields[sweep, pl.ds(0, REACH)] = zero_halo

    @pl.when(jnp.logical_not(has_above))
    def _():
        for sweep in range(SWEEPS):
            fields[sweep, pl.ds(patches + REACH, REACH)] = zero_halo

    acc[...] = jnp.zeros_like(acc)
    first_node = position * span
    low_rows = lax.broadcasted_iota(jnp.int32, (LOW, LANES), 0)

    def add_chunk(slot, k):
        for j in range(pieces):
            local = owners[slot, pl.ds(k * pieces + j, 1), :] - first_node
            high = (local >> 8).astype(jnp.float32).astype(jnp.bfloat16)
            low = local & (LOW - 1)
            lanes = pl.ds(j * LANES, LANES)
            low_hot[:, lanes] = jnp.where(low_rows == low, 1.0, 0.0).astype(jnp.bfloat16)
            vals = values[slot, k, :, lanes]
            high_full = jnp.broadcast_to(high, vals.shape)
            for h in range(highs):
                masked[pl.ds(h * columns, columns), lanes] = jnp.where(
                    high_full == jnp.bfloat16(h), vals, jnp.bfloat16(0)
                )
        acc[...] += lax.dot_general(
            masked[...],
            low_hot[...],
            (((1,), (1,)), ((), ())),
            preferred_element_type=jnp.float32,
        )

    own_owner.wait()

    def step(s, carry):
        is_own = s < chunks
        t = jnp.maximum(s - chunks, 0)
        side = lax.rem(t, 2)
        k = jnp.where(is_own, s, t // 2)
        slot = jnp.where(is_own, 0, 1 + side)

        @pl.when(is_own)
        def _():
            local_load(k).wait()

        from_below = jnp.logical_and(jnp.logical_not(is_own), side == 0)
        from_above = jnp.logical_and(jnp.logical_not(is_own), side == 1)

        @pl.when(jnp.logical_and(from_below, has_below))
        def _():
            @pl.when(t == 0)
            def _():
                owner_copy(0).wait_recv()

            face_copy(0, k).wait_recv()

        @pl.when(jnp.logical_and(from_above, has_above))
        def _():
            @pl.when(t == 1)
            def _():
                owner_copy(1).wait_recv()

            face_copy(1, k).wait_recv()

        present = jnp.logical_or(
            is_own,
            jnp.logical_or(jnp.logical_and(side == 0, has_below), jnp.logical_and(side == 1, has_above)),
        )

        @pl.when(present)
        def _():
            add_chunk(slot, k)

        return carry

    lax.fori_loop(0, 3 * chunks, step, 0)

    def put_surface(h):
        for half in range(LOW // NODES):
            p = h * (LOW // NODES) + half
            patch = acc[pl.ds(h * columns, columns), pl.ds(half * NODES, NODES)]
            patch = patch * weights[NOFF + 2, pl.ds(p, 1), :]
            fields[0, REACH + p] = patch
            surface_stage[:, pl.ds(p * NODES, NODES)] = patch

    def send_halo(sweep):
        @pl.when(has_above)
        def _():
            halo_copy(0, sweep).start()

        @pl.when(has_below)
        def _():
            halo_copy(1, sweep).start()

    def wait_halo(sweep):
        @pl.when(has_below)
        def _():
            halo_copy(0, sweep).wait_recv()

        @pl.when(has_above)
        def _():
            halo_copy(1, sweep).wait_recv()

    ends = REACH * NODES // LOW
    for h in list(range(ends)) + list(range(highs - ends, highs)):
        put_surface(h)
    send_halo(0)
    for h in range(ends, highs - ends):
        put_surface(h)
    surface_copy = pltpu.make_async_copy(surface_stage, surface_out, out_sem.at[0])
    surface_copy.start()

    def relax(sweep, p):
        parts = [weights[at, pl.ds(p, 1), :] for at in range(NOFF + 2)]
        for block in range(columns // 8):
            c = pl.ds(block * 8, 8)
            here = fields[sweep, p + REACH, c, :]
            total = parts[NOFF] * fields[0, p + REACH, c, :]
            total = total + parts[NOFF + 1] * (pltpu.roll(here, 1, 1) + pltpu.roll(here, NODES - 1, 1))
            for at, offset in enumerate(OFFSETS):
                total = total + parts[at] * fields[sweep, p + REACH + offset, c, :]
            if sweep == SWEEPS - 1:
                smooth_stage[c, pl.ds(pl.multiple_of(p * NODES, NODES), NODES)] = total
            else:
                fields[sweep + 1, p + REACH, c, :] = total

    def relax_range(sweep, low, high):
        def one(p, carry):
            relax(sweep, p)
            return carry

        lax.fori_loop(low, high, one, 0)

    for sweep in range(SWEEPS):
        last = sweep == SWEEPS - 1
        if last:
            relax_range(sweep, REACH, patches - REACH)
        wait_halo(sweep)
        relax_range(sweep, 0, REACH)
        relax_range(sweep, patches - REACH, patches)
        if not last:
            send_halo(sweep + 1)
            relax_range(sweep, REACH, patches - REACH)

    smooth_copy = pltpu.make_async_copy(smooth_stage, smooth_out, out_sem.at[1])
    smooth_copy.start()
    surface_copy.wait()
    smooth_copy.wait()

    for side, there in ((0, has_above), (1, has_below)):

        @pl.when(there)
        def _(side=side):
            owner_copy(side).wait_send()
            for k in range(chunks):
                face_copy(side, k).wait_send()
            for sweep in range(SWEEPS):
                halo_copy(side, sweep).wait_send()


def body(sensitivity, owner, patch_count, neighbours, coupling):
    columns, faces = sensitivity.shape
    patches = neighbours.shape[0]
    span = patches * NODES
    chunk = min(1024, faces)
    chunks = faces // chunk
    highs = span // LOW
    any_space = pl.BlockSpec(memory_space=pl.ANY)
    vmem = pl.BlockSpec(memory_space=pltpu.VMEM)
    out = jax.ShapeDtypeStruct((columns, span), jnp.float32)
    dma = pltpu.SemaphoreType.DMA
    return pl.pallas_call(
        functools.partial(kernel, chunk),
        out_shape=(out, out),
        in_specs=[any_space, vmem, pl.BlockSpec(memory_space=pltpu.SMEM), vmem, vmem],
        out_specs=(any_space, any_space),
        scratch_shapes=[
            pltpu.VMEM((3, chunks, columns, chunk), jnp.bfloat16),
            pltpu.VMEM((3, faces // LANES, LANES), jnp.int32),
            pltpu.VMEM((highs * columns, chunk), jnp.bfloat16),
            pltpu.VMEM((LOW, chunk), jnp.bfloat16),
            pltpu.VMEM((highs * columns, LOW), jnp.float32),
            pltpu.VMEM((SWEEPS, patches + 2 * REACH, columns, NODES), jnp.float32),
            pltpu.VMEM((NOFF + 3, patches, LANES), jnp.float32),
            pltpu.VMEM((columns, span), jnp.float32),
            pltpu.VMEM((columns, span), jnp.float32),
            dma((chunks,)),
            dma,
            dma((2, chunks)),
            dma((2, chunks)),
            dma((2,)),
            dma((2,)),
            dma((2, SWEEPS)),
            dma((2, SWEEPS)),
            dma((2,)),
        ],
        compiler_params=pltpu.CompilerParams(
            collective_id=0, has_side_effects=True, vmem_limit_bytes=48 * 1024 * 1024
        ),
    )(sensitivity, owner.reshape(faces // LANES, LANES), patch_count, neighbours, coupling)


def solution(mesh):
    placed = (
        P(None, ("groups", "surf")),
        P(("groups", "surf")),
        P(("groups", "surf")),
        P(("groups", "surf"), None),
        P(("groups", "surf"), None),
    )
    return jax.shard_map(
        body,
        mesh=mesh,
        in_specs=placed,
        out_specs=(P(None, ("groups", "surf")), P(None, ("groups", "surf"))),
        check_vma=False,
    )
```

```python
import functools

import jax
import jax.numpy as jnp
from jax import lax
from jax.experimental import pallas as pl
from jax.experimental.pallas import tpu as pltpu
from jax.sharding import PartitionSpec as P

NODES = 128
REACH = 4
SWEEPS = 4
LOW = 256
LANES = 128
smoothing = 1.5
OFFSETS = [d for d in range(-REACH, REACH + 1) if d != 0]
NOFF = len(OFFSETS)
MESH = pl.DeviceIdType.MESH


def kernel(
    chunk,
    sens,
    owner,
    count,
    neighbours_in,
    coupling_in,
    surface_out,
    smooth_out,
    neighbours,
    coupling,
    link_sem,
    values,
    owners,
    masked,
    low_hot,
    acc,
    fields,
    weights,
    table,
    halo_out,
    halo_in,
    surface_stage,
    smooth_stage,
    out_sem,
    load_sem,
    oload_sem,
    send_sem,
    recv_sem,
    osend_sem,
    orecv_sem,
    hsend_sem,
    hrecv_sem,
):
    columns, faces = sens.shape
    patches = neighbours.shape[1]
    span = patches * NODES
    highs = span // LOW
    chunks = faces // chunk
    pieces = chunk // LANES
    orow = faces // LANES
    position = lax.axis_index("surf")
    peers = lax.axis_size("surf")
    has_below = position > 0
    has_above = position < peers - 1

    def local_load(k):
        return pltpu.make_async_copy(sens.at[:, pl.ds(k * chunk, chunk)], values.at[0, k], load_sem.at[k])

    def face_copy(side, k):
        target = position + 1 if side == 0 else position - 1
        return pltpu.make_async_remote_copy(
            src_ref=sens.at[:, pl.ds(k * chunk, chunk)],
            dst_ref=values.at[1 + side, k],
            send_sem=send_sem.at[side, k],
            recv_sem=recv_sem.at[side, k],
            device_id={"surf": target},
            device_id_type=MESH,
        )

    def owner_copy(side):
        target = position + 1 if side == 0 else position - 1
        return pltpu.make_async_remote_copy(
            src_ref=owner,
            dst_ref=owners.at[1 + side],
            send_sem=osend_sem.at[side],
            recv_sem=orecv_sem.at[side],
            device_id={"surf": target},
            device_id_type=MESH,
        )

    def halo_copy(side, sweep):
        target = position + 1 if side == 0 else position - 1
        if sweep == SWEEPS - 1:
            source = patches if side == 0 else REACH
            landing = 0 if side == 0 else patches + REACH
            src, dst = fields.at[sweep, pl.ds(source, REACH)], fields.at[sweep, pl.ds(landing, REACH)]
        else:
            src, dst = halo_out.at[side, sweep], halo_in.at[side, sweep]
        return pltpu.make_async_remote_copy(
            src_ref=src,
            dst_ref=dst,
            send_sem=hsend_sem.at[side, sweep],
            recv_sem=hrecv_sem.at[side, sweep],
            device_id={"surf": target},
            device_id_type=MESH,
        )

    own_owner = pltpu.make_async_copy(owner, owners.at[0], oload_sem)
    own_owner.start()
    link_copies = (
        pltpu.make_async_copy(neighbours_in, neighbours, link_sem.at[0]),
        pltpu.make_async_copy(coupling_in, coupling, link_sem.at[1]),
    )
    for link_copy in link_copies:
        link_copy.start()
    for k in range(chunks):
        local_load(k).start()

    barrier = pltpu.get_barrier_semaphore()

    @pl.when(has_below)
    def _():
        pl.semaphore_signal(barrier, inc=1, device_id={"surf": position - 1}, device_id_type=MESH)

    @pl.when(has_above)
    def _():
        pl.semaphore_signal(barrier, inc=1, device_id={"surf": position + 1}, device_id_type=MESH)

    both = jnp.logical_and(has_below, has_above)

    @pl.when(both)
    def _():
        pl.semaphore_wait(barrier, 2)

    @pl.when(jnp.logical_not(both))
    def _():
        pl.semaphore_wait(barrier, 1)

    @pl.when(has_above)
    def _():
        owner_copy(0).start()

    @pl.when(has_below)
    def _():
        owner_copy(1).start()

    for k in range(chunks):

        @pl.when(has_above)
        def _(k=k):
            face_copy(0, k).start()

        @pl.when(has_below)
        def _(k=k):
            face_copy(1, k).start()

    for link_copy in link_copies:
        link_copy.wait()
    slots = lax.broadcasted_iota(jnp.int32, neighbours.shape, 1)
    distance = neighbours[...] - (position * patches + slots)
    links = coupling[...]
    along = lax.broadcasted_iota(jnp.int32, (1, patches), 1)
    alive = jnp.where(along < count[0], 1.0, 0.0).astype(jnp.float32)
    share = alive / (1.0 + smoothing * (2.0 + jnp.sum(links, axis=0, keepdims=True)))
    lines = [
        smoothing * share * jnp.sum(jnp.where(distance == offset, links, 0.0), axis=0, keepdims=True)
        for offset in OFFSETS
    ]
    lines += [share, smoothing * share, alive]
    table[...] = jnp.zeros_like(table)
    for at, line in enumerate(lines):
        table[pl.ds(at, 1), pl.ds(0, patches)] = line
    turned = jnp.transpose(table[...])
    for at in range(len(lines)):
        weights[at] = jnp.broadcast_to(turned[0:patches, at : at + 1], (patches, LANES))

    zero_halo = jnp.zeros((REACH, columns, NODES), jnp.float32)

    @pl.when(jnp.logical_not(has_below))
    def _():
        for sweep in range(SWEEPS):
            fields[sweep, pl.ds(0, REACH)] = zero_halo

    @pl.when(jnp.logical_not(has_above))
    def _():
        for sweep in range(SWEEPS):
            fields[sweep, pl.ds(patches + REACH, REACH)] = zero_halo

    acc[...] = jnp.zeros_like(acc)
    first_node = position * span
    low_rows = lax.broadcasted_iota(jnp.int32, (LOW, LANES), 0)

    def add_chunk(slot, k):
        for j in range(pieces):
            local = owners[slot, pl.ds(k * pieces + j, 1), :] - first_node
            high = (local >> 8).astype(jnp.float32).astype(jnp.bfloat16)
            low = local & (LOW - 1)
            lanes = pl.ds(j * LANES, LANES)
            low_hot[:, lanes] = jnp.where(low_rows == low, 1.0, 0.0).astype(jnp.bfloat16)
            vals = values[slot, k, :, lanes]
            high_full = jnp.broadcast_to(high, vals.shape)
            for h in range(highs):
                masked[pl.ds(h * columns, columns), lanes] = jnp.where(
                    high_full == jnp.bfloat16(h), vals, jnp.bfloat16(0)
                )
        acc[...] += lax.dot_general(
            masked[...],
            low_hot[...],
            (((1,), (1,)), ((), ())),
            preferred_element_type=jnp.float32,
        )

    own_owner.wait()

    def step(s, carry):
        is_own = s < chunks
        t = jnp.maximum(s - chunks, 0)
        side = lax.rem(t, 2)
        k = jnp.where(is_own, s, t // 2)
        slot = jnp.where(is_own, 0, 1 + side)

        @pl.when(is_own)
        def _():
            local_load(k).wait()

        from_below = jnp.logical_and(jnp.logical_not(is_own), side == 0)
        from_above = jnp.logical_and(jnp.logical_not(is_own), side == 1)

        @pl.when(jnp.logical_and(from_below, has_below))
        def _():
            @pl.when(t == 0)
            def _():
                owner_copy(0).wait_recv()

            face_copy(0, k).wait_recv()

        @pl.when(jnp.logical_and(from_above, has_above))
        def _():
            @pl.when(t == 1)
            def _():
                owner_copy(1).wait_recv()

            face_copy(1, k).wait_recv()

        present = jnp.logical_or(
            is_own,
            jnp.logical_or(jnp.logical_and(side == 0, has_below), jnp.logical_and(side == 1, has_above)),
        )

        @pl.when(present)
        def _():
            add_chunk(slot, k)

        return carry

    lax.fori_loop(0, 3 * chunks, step, 0)

    def put_surface(h):
        for half in range(LOW // NODES):
            p = h * (LOW // NODES) + half
            patch = acc[pl.ds(h * columns, columns), pl.ds(half * NODES, NODES)]
            patch = patch * weights[NOFF + 2, pl.ds(p, 1), :]
            fields[0, REACH + p] = patch
            surface_stage[:, pl.ds(p * NODES, NODES)] = patch

    def send_halo(sweep):
        for side, there in ((0, has_above), (1, has_below)):

            @pl.when(there)
            def _(side=side):
                if sweep < SWEEPS - 1:
                    first = patches if side == 0 else REACH
                    halo_out[side, sweep] = fields[sweep, pl.ds(first, REACH)].astype(jnp.bfloat16)
                halo_copy(side, sweep).start()

    def wait_halo(sweep):
        for side, there in ((0, has_below), (1, has_above)):

            @pl.when(there)
            def _(side=side):
                halo_copy(side, sweep).wait_recv()
                if sweep < SWEEPS - 1:
                    first = 0 if side == 0 else patches + REACH
                    fields[sweep, pl.ds(first, REACH)] = halo_in[side, sweep].astype(jnp.float32)

    ends = REACH * NODES // LOW
    for h in list(range(ends)) + list(range(highs - ends, highs)):
        put_surface(h)
    send_halo(0)
    for h in range(ends, highs - ends):
        put_surface(h)

    surface_copy = pltpu.make_async_copy(surface_stage, surface_out, out_sem.at[0])
    surface_copy.start()

    def relax(sweep, p):
        parts = [weights[at, pl.ds(p, 1), :] for at in range(NOFF + 2)]
        for block in range(columns // 8):
            c = pl.ds(block * 8, 8)
            here = fields[sweep, p + REACH, c, :]
            total = parts[NOFF] * fields[0, p + REACH, c, :]
            total = total + parts[NOFF + 1] * (pltpu.roll(here, 1, 1) + pltpu.roll(here, NODES - 1, 1))
            for at, offset in enumerate(OFFSETS):
                total = total + parts[at] * fields[sweep, p + REACH + offset, c, :]
            if sweep == SWEEPS - 1:
                smooth_stage[c, pl.ds(pl.multiple_of(p * NODES, NODES), NODES)] = total
            else:
                fields[sweep + 1, p + REACH, c, :] = total

    def relax_range(sweep, low, high):
        def one(p, carry):
            relax(sweep, p)
            return carry

        lax.fori_loop(low, high, one, 0)

    for sweep in range(SWEEPS):
        last = sweep == SWEEPS - 1
        if last:
            relax_range(sweep, REACH, patches - REACH)
        wait_halo(sweep)
        relax_range(sweep, 0, REACH)
        relax_range(sweep, patches - REACH, patches)
        if not last:
            send_halo(sweep + 1)
            relax_range(sweep, REACH, patches - REACH)

    smooth_copy = pltpu.make_async_copy(smooth_stage, smooth_out, out_sem.at[1])
    smooth_copy.start()
    surface_copy.wait()
    smooth_copy.wait()

    for side, there in ((0, has_above), (1, has_below)):

        @pl.when(there)
        def _(side=side):
            owner_copy(side).wait_send()
            for k in range(chunks):
                face_copy(side, k).wait_send()
            for sweep in range(SWEEPS):
                halo_copy(side, sweep).wait_send()


def body(sensitivity, owner, patch_count, neighbours, coupling):
    columns, faces = sensitivity.shape
    patches = neighbours.shape[0]
    span = patches * NODES
    chunk = min(512, faces)
    chunks = faces // chunk
    highs = span // LOW
    hbm = pl.BlockSpec(memory_space=pltpu.HBM)
    vmem = pl.BlockSpec(memory_space=pltpu.VMEM)
    links = neighbours.T.shape
    out = jax.ShapeDtypeStruct((columns, span), jnp.float32)
    dma = pltpu.SemaphoreType.DMA
    return pl.pallas_call(
        functools.partial(kernel, chunk),
        out_shape=(out, out),
        in_specs=[hbm, hbm, pl.BlockSpec(memory_space=pltpu.SMEM), hbm, hbm],
        out_specs=(hbm, hbm),
        scratch_shapes=[
            pltpu.VMEM(links, jnp.int32),
            pltpu.VMEM(links, jnp.float32),
            dma((2,)),
            pltpu.VMEM((3, chunks, columns, chunk), jnp.bfloat16),
            pltpu.VMEM((3, faces // LANES, LANES), jnp.int32),
            pltpu.VMEM((highs * columns, chunk), jnp.bfloat16),
            pltpu.VMEM((LOW, chunk), jnp.bfloat16),
            pltpu.VMEM((highs * columns, LOW), jnp.float32),
            pltpu.VMEM((SWEEPS, patches + 2 * REACH, columns, NODES), jnp.float32),
            pltpu.VMEM((NOFF + 3, patches, LANES), jnp.float32),
            pltpu.VMEM((16, LANES), jnp.float32),
            pltpu.VMEM((2, SWEEPS - 1, REACH, columns, NODES), jnp.bfloat16),
            pltpu.VMEM((2, SWEEPS - 1, REACH, columns, NODES), jnp.bfloat16),
            pltpu.VMEM((columns, span), jnp.float32),
            pltpu.VMEM((columns, span), jnp.float32),
            dma((2,)),
            dma((chunks,)),
            dma,
            dma((2, chunks)),
            dma((2, chunks)),
            dma((2,)),
            dma((2,)),
            dma((2, SWEEPS)),
            dma((2, SWEEPS)),
        ],
        compiler_params=pltpu.CompilerParams(
            collective_id=0, has_side_effects=True, vmem_limit_bytes=63 * 1024 * 1024
        ),
    )(sensitivity, owner.reshape(faces // LANES, LANES), patch_count, neighbours.T, coupling.T)


def solution(mesh):
    placed = (
        P(None, ("groups", "surf")),
        P(("groups", "surf")),
        P(("groups", "surf")),
        P(("groups", "surf"), None),
        P(("groups", "surf"), None),
    )
    return jax.shard_map(
        body,
        mesh=mesh,
        in_specs=placed,
        out_specs=(P(None, ("groups", "surf")), P(None, ("groups", "surf"))),
        check_vma=False,
    )
```

```python
import functools

import jax
import jax.numpy as jnp
from jax import lax
from jax.experimental import pallas as pl
from jax.experimental.pallas import tpu as pltpu
from jax.sharding import PartitionSpec as P

NODES = 128
REACH = 4
SWEEPS = 4
LOW = 256
LANES = 128
SPLIT = 4
smoothing = 1.5
OFFSETS = [d for d in range(-REACH, REACH + 1) if d != 0]
NOFF = len(OFFSETS)
MESH = pl.DeviceIdType.MESH


def kernel(
    chunk,
    sens,
    owner,
    count,
    neighbours_in,
    coupling_in,
    surface_out,
    smooth_out,
    neighbours,
    coupling,
    link_sem,
    values,
    owners,
    masked,
    low_hot,
    acc,
    fields,
    weights,
    table,
    halo_out,
    halo_in,
    surface_stage,
    smooth_stage,
    out_sem,
    load_sem,
    oload_sem,
    send_sem,
    recv_sem,
    osend_sem,
    orecv_sem,
    hsend_sem,
    hrecv_sem,
):
    columns, faces = sens.shape
    patches = neighbours.shape[1]
    span = patches * NODES
    highs = span // LOW
    chunks = faces // chunk
    pieces = chunk // LANES
    orow = faces // LANES
    position = lax.axis_index("surf")
    peers = lax.axis_size("surf")
    has_below = position > 0
    has_above = position < peers - 1

    def local_load(k):
        return pltpu.make_async_copy(sens.at[:, pl.ds(k * chunk, chunk)], values.at[0, k], load_sem.at[k])

    def face_copy(side, k):
        target = position + 1 if side == 0 else position - 1
        return pltpu.make_async_remote_copy(
            src_ref=sens.at[:, pl.ds(k * chunk, chunk)],
            dst_ref=values.at[1 + side, k],
            send_sem=send_sem.at[side, k],
            recv_sem=recv_sem.at[side, k],
            device_id={"surf": target},
            device_id_type=MESH,
        )

    def owner_copy(side):
        target = position + 1 if side == 0 else position - 1
        return pltpu.make_async_remote_copy(
            src_ref=owner,
            dst_ref=owners.at[1 + side],
            send_sem=osend_sem.at[side],
            recv_sem=orecv_sem.at[side],
            device_id={"surf": target},
            device_id_type=MESH,
        )

    def halo_copy(side, sweep):
        target = position + 1 if side == 0 else position - 1
        if sweep == SWEEPS - 1:
            source = patches if side == 0 else REACH
            landing = 0 if side == 0 else patches + REACH
            src, dst = fields.at[sweep, pl.ds(source, REACH)], fields.at[sweep, pl.ds(landing, REACH)]
        else:
            src, dst = halo_out.at[side, sweep], halo_in.at[side, sweep]
        return pltpu.make_async_remote_copy(
            src_ref=src,
            dst_ref=dst,
            send_sem=hsend_sem.at[side, sweep],
            recv_sem=hrecv_sem.at[side, sweep],
            device_id={"surf": target},
            device_id_type=MESH,
        )

    own_owner = pltpu.make_async_copy(owner, owners.at[0], oload_sem)
    own_owner.start()
    link_copies = (
        pltpu.make_async_copy(neighbours_in, neighbours, link_sem.at[0]),
        pltpu.make_async_copy(coupling_in, coupling, link_sem.at[1]),
    )
    for link_copy in link_copies:
        link_copy.start()
    for k in range(chunks):
        local_load(k).start()

    barrier = pltpu.get_barrier_semaphore()

    @pl.when(has_below)
    def _():
        pl.semaphore_signal(barrier, inc=1, device_id={"surf": position - 1}, device_id_type=MESH)

    @pl.when(has_above)
    def _():
        pl.semaphore_signal(barrier, inc=1, device_id={"surf": position + 1}, device_id_type=MESH)

    both = jnp.logical_and(has_below, has_above)

    @pl.when(both)
    def _():
        pl.semaphore_wait(barrier, 2)

    @pl.when(jnp.logical_not(both))
    def _():
        pl.semaphore_wait(barrier, 1)

    @pl.when(has_above)
    def _():
        owner_copy(0).start()

    @pl.when(has_below)
    def _():
        owner_copy(1).start()

    for k in range(chunks):

        @pl.when(has_above)
        def _(k=k):
            face_copy(0, k).start()

        @pl.when(has_below)
        def _(k=k):
            face_copy(1, k).start()

    for link_copy in link_copies:
        link_copy.wait()
    slots = lax.broadcasted_iota(jnp.int32, neighbours.shape, 1)
    distance = neighbours[...] - (position * patches + slots)
    links = coupling[...]
    along = lax.broadcasted_iota(jnp.int32, (1, patches), 1)
    alive = jnp.where(along < count[0], 1.0, 0.0).astype(jnp.float32)
    share = alive / (1.0 + smoothing * (2.0 + jnp.sum(links, axis=0, keepdims=True)))
    lines = [
        smoothing * share * jnp.sum(jnp.where(distance == offset, links, 0.0), axis=0, keepdims=True)
        for offset in OFFSETS
    ]
    lines += [share, smoothing * share, alive]
    table[...] = jnp.zeros_like(table)
    for at, line in enumerate(lines):
        table[pl.ds(at, 1), pl.ds(0, patches)] = line
    turned = jnp.transpose(table[...])
    for at in range(len(lines)):
        weights[at] = jnp.broadcast_to(turned[0:patches, at : at + 1], (patches, LANES))

    zero_halo = jnp.zeros((REACH, columns, NODES), jnp.float32)

    @pl.when(jnp.logical_not(has_below))
    def _():
        for sweep in range(SWEEPS):
            fields[sweep, pl.ds(0, REACH)] = zero_halo

    @pl.when(jnp.logical_not(has_above))
    def _():
        for sweep in range(SWEEPS):
            fields[sweep, pl.ds(patches + REACH, REACH)] = zero_halo

    acc[...] = jnp.zeros_like(acc)
    first_node = position * span
    low_rows = lax.broadcasted_iota(jnp.int32, (LOW, LANES), 0)

    def add_chunk(slot, k):
        for j in range(pieces):
            local = owners[slot, pl.ds(k * pieces + j, 1), :] - first_node
            high = (local >> 8).astype(jnp.float32).astype(jnp.bfloat16)
            low = local & (LOW - 1)
            lanes = pl.ds(j * LANES, LANES)
            low_hot[:, lanes] = jnp.where(low_rows == low, 1.0, 0.0).astype(jnp.bfloat16)
            vals = values[slot, k, :, lanes]
            high_full = jnp.broadcast_to(high, vals.shape)
            for h in range(highs):
                masked[pl.ds(h * columns, columns), lanes] = jnp.where(
                    high_full == jnp.bfloat16(h), vals, jnp.bfloat16(0)
                )
        acc[...] += lax.dot_general(
            masked[...],
            low_hot[...],
            (((1,), (1,)), ((), ())),
            preferred_element_type=jnp.float32,
        )

    own_owner.wait()

    def step(s, carry):
        is_own = s < chunks
        t = jnp.maximum(s - chunks, 0)
        side = lax.rem(t, 2)
        k = jnp.where(is_own, s, t // 2)
        slot = jnp.where(is_own, 0, 1 + side)

        @pl.when(is_own)
        def _():
            local_load(k).wait()

        from_below = jnp.logical_and(jnp.logical_not(is_own), side == 0)
        from_above = jnp.logical_and(jnp.logical_not(is_own), side == 1)

        @pl.when(jnp.logical_and(from_below, has_below))
        def _():
            @pl.when(t == 0)
            def _():
                owner_copy(0).wait_recv()

            face_copy(0, k).wait_recv()

        @pl.when(jnp.logical_and(from_above, has_above))
        def _():
            @pl.when(t == 1)
            def _():
                owner_copy(1).wait_recv()

            face_copy(1, k).wait_recv()

        present = jnp.logical_or(
            is_own,
            jnp.logical_or(jnp.logical_and(side == 0, has_below), jnp.logical_and(side == 1, has_above)),
        )

        @pl.when(present)
        def _():
            add_chunk(slot, k)

        return carry

    lax.fori_loop(0, 3 * chunks, step, 0)

    def put_surface(h):
        for half in range(LOW // NODES):
            p = h * (LOW // NODES) + half
            patch = acc[pl.ds(h * columns, columns), pl.ds(half * NODES, NODES)]
            patch = patch * weights[NOFF + 2, pl.ds(p, 1), :]
            fields[0, REACH + p] = patch
            surface_stage[:, pl.ds(p * NODES, NODES)] = patch

    def send_halo(sweep):
        for side, there in ((0, has_above), (1, has_below)):

            @pl.when(there)
            def _(side=side):
                if sweep < SWEEPS - 1:
                    first = patches if side == 0 else REACH
                    halo_out[side, sweep] = fields[sweep, pl.ds(first, REACH)].astype(jnp.bfloat16)
                halo_copy(side, sweep).start()

    def wait_halo(sweep):
        for side, there in ((0, has_below), (1, has_above)):

            @pl.when(there)
            def _(side=side):
                halo_copy(side, sweep).wait_recv()
                if sweep < SWEEPS - 1:
                    first = 0 if side == 0 else patches + REACH
                    fields[sweep, pl.ds(first, REACH)] = halo_in[side, sweep].astype(jnp.float32)

    ends = REACH * NODES // LOW
    for h in list(range(ends)) + list(range(highs - ends, highs)):
        put_surface(h)
    send_halo(0)
    for h in range(ends, highs - ends):
        put_surface(h)

    surface_copy = pltpu.make_async_copy(surface_stage, surface_out, out_sem.at[0])
    surface_copy.start()

    def relax(sweep, p):
        parts = [weights[at, pl.ds(p, 1), :] for at in range(NOFF + 2)]
        for block in range(columns // 8):
            c = pl.ds(block * 8, 8)
            here = fields[sweep, p + REACH, c, :]
            total = parts[NOFF] * fields[0, p + REACH, c, :]
            total = total + parts[NOFF + 1] * (pltpu.roll(here, 1, 1) + pltpu.roll(here, NODES - 1, 1))
            for at, offset in enumerate(OFFSETS):
                total = total + parts[at] * fields[sweep, p + REACH + offset, c, :]
            if sweep == SWEEPS - 1:
                smooth_stage[c, pl.ds(pl.multiple_of(p * NODES, NODES), NODES)] = total
            else:
                fields[sweep + 1, p + REACH, c, :] = total

    def relax_range(sweep, low, high):
        def one(p, carry):
            relax(sweep, p)
            return carry

        lax.fori_loop(low, high, one, 0)

    for sweep in range(SWEEPS):
        last = sweep == SWEEPS - 1
        if last:
            relax_range(sweep, REACH, patches - REACH)
        wait_halo(sweep)
        relax_range(sweep, 0, REACH)
        relax_range(sweep, patches - REACH, patches)
        if not last:
            send_halo(sweep + 1)
            relax_range(sweep, REACH, patches - REACH)

    smooth_copy = pltpu.make_async_copy(smooth_stage, smooth_out, out_sem.at[1])
    smooth_copy.start()
    surface_copy.wait()
    smooth_copy.wait()

    for side, there in ((0, has_above), (1, has_below)):

        @pl.when(there)
        def _(side=side):
            owner_copy(side).wait_send()
            for k in range(chunks):
                face_copy(side, k).wait_send()
            for sweep in range(SWEEPS):
                halo_copy(side, sweep).wait_send()


def hand_over(surface, smooth, surface_out, smooth_out, stage, in_sem, out_sem):
    step = surface.shape[0] // SPLIT
    fetches, stores = [], []
    for at, (source, target) in enumerate(((surface, surface_out), (smooth, smooth_out))):
        for k in range(SPLIT):
            rows = pl.ds(k * step, step)
            fetches.append(pltpu.make_async_copy(source.at[rows], stage.at[at, rows], in_sem.at[at, k]))
            stores.append(pltpu.make_async_copy(stage.at[at, rows], target.at[rows], out_sem.at[at, k]))
    for fetch in fetches:
        fetch.start()
    for fetch, store in zip(fetches, stores):
        fetch.wait()
        store.start()
    for store in stores:
        store.wait()


def body(sensitivity, owner, patch_count, neighbours, coupling):
    columns, faces = sensitivity.shape
    patches = neighbours.shape[0]
    span = patches * NODES
    chunk = min(512, faces)
    chunks = faces // chunk
    highs = span // LOW
    hbm = pl.BlockSpec(memory_space=pltpu.HBM)
    vmem = pl.BlockSpec(memory_space=pltpu.VMEM)
    links = neighbours.T.shape
    out = jax.ShapeDtypeStruct((columns, span), jnp.float32)
    dma = pltpu.SemaphoreType.DMA
    outputs = pl.pallas_call(
        functools.partial(kernel, chunk),
        out_shape=(out, out),
        in_specs=[hbm, hbm, pl.BlockSpec(memory_space=pltpu.SMEM), hbm, hbm],
        out_specs=(hbm, hbm),
        scratch_shapes=[
            pltpu.VMEM(links, jnp.int32),
            pltpu.VMEM(links, jnp.float32),
            dma((2,)),
            pltpu.VMEM((3, chunks, columns, chunk), jnp.bfloat16),
            pltpu.VMEM((3, faces // LANES, LANES), jnp.int32),
            pltpu.VMEM((highs * columns, chunk), jnp.bfloat16),
            pltpu.VMEM((LOW, chunk), jnp.bfloat16),
            pltpu.VMEM((highs * columns, LOW), jnp.float32),
            pltpu.VMEM((SWEEPS, patches + 2 * REACH, columns, NODES), jnp.float32),
            pltpu.VMEM((NOFF + 3, patches, LANES), jnp.float32),
            pltpu.VMEM((16, LANES), jnp.float32),
            pltpu.VMEM((2, SWEEPS - 1, REACH, columns, NODES), jnp.bfloat16),
            pltpu.VMEM((2, SWEEPS - 1, REACH, columns, NODES), jnp.bfloat16),
            pltpu.VMEM((columns, span), jnp.float32),
            pltpu.VMEM((columns, span), jnp.float32),
            dma((2,)),
            dma((chunks,)),
            dma,
            dma((2, chunks)),
            dma((2, chunks)),
            dma((2,)),
            dma((2,)),
            dma((2, SWEEPS)),
            dma((2, SWEEPS)),
        ],
        compiler_params=pltpu.CompilerParams(
            collective_id=0, has_side_effects=True, vmem_limit_bytes=63 * 1024 * 1024
        ),
    )(sensitivity, owner.reshape(faces // LANES, LANES), patch_count, neighbours.T, coupling.T)
    return pl.pallas_call(
        hand_over,
        out_shape=(out, out),
        in_specs=[hbm, hbm],
        out_specs=(hbm, hbm),
        scratch_shapes=[pltpu.VMEM((2, columns, span), jnp.float32), dma((2, SPLIT)), dma((2, SPLIT))],
        compiler_params=pltpu.CompilerParams(vmem_limit_bytes=63 * 1024 * 1024),
    )(*outputs)


def solution(mesh):
    placed = (
        P(None, ("groups", "surf")),
        P(("groups", "surf")),
        P(("groups", "surf")),
        P(("groups", "surf"), None),
        P(("groups", "surf"), None),
    )
    return jax.shard_map(
        body,
        mesh=mesh,
        in_specs=placed,
        out_specs=(P(None, ("groups", "surf")), P(None, ("groups", "surf"))),
        check_vma=False,
    )
```
